512 devices in a mesh: dp: 256 (over z, x_hi, y, core), rep: 2 (over x_lo).
Axes of the slice: x: 4 (x_hi: 2, x_lo: 2; x = x_hi * 2 + x_lo), y: 8, z: 8, core: 2. Of those that a mesh axis runs over, the one named last changes fastest.
Arguments:
- features: bfloat16 [65536, 1152], P('dp'), may hold values from -0.046875 to 0.046875
- img_weight: bfloat16 [1152, 1152], P(None, 'rep'), may hold values from -4 to 4
- text_embed: bfloat16 [65536, 1152], P('dp', 'rep'), may hold values from -0.4375 to 0.4375
- log_scale: float32 [1], replicated, may hold values from 1.6 to 2.6
- logit_bias: float32 [1], replicated, may hold values from -4 to -1
Outputs:
- image_grad: bfloat16 [65536, 1152], P('dp', 'rep')
- text_grad: bfloat16 [65536, 1152], P('dp', 'rep')
- weight_grad: bfloat16 [1152, 1152], P(None, 'rep')
The draws below stay inside these ranges and needn't reach their ends.
All inputs are finite; a program needn't handle non-finite values.
Results may differ from the reference program's by a relative error of at most 0.017.
Values may be sent and summed in bfloat16 or wider, within the bound.
No kernel may reach another device: no remote copies, remote signals or barrier semaphores. Data moves between devices by JAX's collectives and lax.ppermute only.
A program may use at most 64 MiB of HBM per device.

```python
import jax
import jax.numpy as jnp
from jax import lax

D = 1152
E = 1152
TOK_DEV = 256
STEPS = 4
TOKENS = 65536
N_DP = 256


def shard_levels(stream_key, extent, split, least, largest):
    def one(position, blocks):
        heights = jax.random.uniform(jax.random.fold_in(jax.random.fold_in(stream_key, 6), position), (blocks,), jnp.float32, least / len(split), largest / len(split))
        return jnp.repeat(jnp.exp(heights), extent[position] // blocks).reshape((-1,) + (1,) * (len(extent) - position - 1))

    loudness = one(*split[0])
    for cut in split[1:]:
        loudness = loudness * one(*cut)
    return loudness


def noise(key, dims, width, most, shards=(), held_as=jnp.bfloat16):
    values = width * jax.random.normal(key, dims, jnp.float32)
    if shards:
        values = values * shard_levels(key, dims, shards, -0.22, 0.18)
    return jnp.clip(values, -most, most).astype(held_as)


def setup_inputs(seed: int = 0) -> dict:
    splits = jax.random.split(jax.random.key(seed), 6)
    return {
        "features": noise(splits[0], (TOKENS, D), 0.003, 0.046875, ((0, 256),)),
        "img_weight": noise(splits[1], (D, E), 0.3, 4.0, ((1, 2),)),
        "text_embed": noise(splits[2], (TOKENS, E), 0.03, 0.4375, ((0, 256), (1, 2))),
        "log_scale": jnp.clip(jax.random.uniform(splits[3], (1,), jnp.float32, 1.6, 2.6), 1.6, 2.6),
        "logit_bias": jnp.clip(jax.random.uniform(splits[4], (1,), jnp.float32, -4.0, -1.0), -4.0, -1.0),
    }


epsilon = 1e-06

def reference(features, img_weight, text_embed, log_scale, logit_bias):
    logit_scale = jnp.exp(log_scale[0])
    offset_value = logit_bias[0]
    img_raw = jnp.dot(features, img_weight, preferred_element_type=jnp.float32)
    img_inv = lax.rsqrt(lax.optimization_barrier(jnp.sum(img_raw * img_raw, axis=1, keepdims=True)) + epsilon)
    img_hat = img_raw * img_inv
    txt_raw = text_embed.astype(jnp.float32)
    txt_inv = lax.rsqrt(lax.optimization_barrier(jnp.sum(txt_raw * txt_raw, axis=1, keepdims=True)) + epsilon)
    txt_hat = txt_raw * txt_inv
    img_blocks = lax.optimization_barrier(img_hat.astype(jnp.bfloat16)).astype(jnp.float32).reshape(N_DP, TOK_DEV, E)
    txt_blocks = lax.optimization_barrier(txt_hat.astype(jnp.bfloat16)).astype(jnp.float32).reshape(N_DP, TOK_DEV, E)
    positives = jnp.eye(TOK_DEV, dtype=jnp.float32)
    grad_img = jnp.zeros((N_DP, TOK_DEV, E), jnp.float32)
    grad_txt = jnp.zeros((N_DP, TOK_DEV, E), jnp.float32)
    for stride in range(STEPS + 1):
        text_span = jnp.roll(txt_blocks, stride, axis=0)
        logits = logit_scale * jnp.einsum('kie,kje->kij', img_blocks, text_span) + offset_value
        sig_grad = jax.nn.sigmoid(logits)
        if stride == 0:
            sig_grad = sig_grad - positives
        grad_bf = lax.optimization_barrier(sig_grad.astype(jnp.bfloat16)).astype(jnp.float32)
        grad_img = grad_img + logit_scale * jnp.einsum('kij,kje->kie', grad_bf, text_span)
        contrib = logit_scale * jnp.einsum('kij,kie->kje', grad_bf, img_blocks)
        grad_txt = grad_txt + jnp.roll(contrib, -stride, axis=0)
    grad_img = grad_img.reshape(TOKENS, E)
    grad_txt = grad_txt.reshape(TOKENS, E)
    img_dot = lax.optimization_barrier(jnp.sum(img_hat * grad_img, axis=1, keepdims=True))
    txt_dot = lax.optimization_barrier(jnp.sum(txt_hat * grad_txt, axis=1, keepdims=True))
    image_grad = ((grad_img - img_hat * img_dot) * img_inv).astype(jnp.bfloat16)
    text_grad = ((grad_txt - txt_hat * txt_dot) * txt_inv).astype(jnp.bfloat16)
    weight_grad = jnp.dot(features.T, image_grad, preferred_element_type=jnp.float32).astype(jnp.bfloat16)
    return (image_grad, text_grad, weight_grad)
```

```python
import jax
import jax.numpy as jnp
from jax import lax
from jax.sharding import Mesh, PartitionSpec as P

STEPS = 4
AXES = ("z", "xh", "y", "core", "rep")
DP = ("z", "xh", "y", "core")
PLANE = ("z", "y")

epsilon = 1e-06


def passed_along(array, by):
    peers = 256
    return lax.ppermute(array, DP, [(i, (i + by) % peers) for i in range(peers)])


def swapped(array, axis):
    return lax.ppermute(array, axis, [(0, 1), (1, 0)])


def weight_sum(features, image_grad):
    peers = lax.axis_size(PLANE)
    core = lax.axis_index("core")
    grad_t = image_grad.T
    part = grad_t.shape[0] // 2
    width = features.shape[1]
    mine = lax.dynamic_slice_in_dim(grad_t, core * part, part, 0)
    theirs = lax.dynamic_slice_in_dim(grad_t, (1 - core) * part, part, 0)
    received = swapped(theirs, "core")
    other_features = swapped(features, "core")
    total = jnp.dot(mine, features, preferred_element_type=jnp.float32) + jnp.dot(
        received, other_features, preferred_element_type=jnp.float32
    )
    groups = width // 128
    rows = groups * part
    tiles = total.astype(jnp.bfloat16).reshape(part, groups, 128).transpose(1, 0, 2).reshape(rows, 128)
    deep = -(-rows // (peers * 16)) * 16
    tiles = jnp.pad(tiles, ((0, peers * deep - rows), (0, 0))).reshape(peers, deep, 128)
    pieces = lax.all_to_all(tiles, PLANE, 0, 0, tiled=True)
    piece = jnp.sum(pieces.astype(jnp.float32), axis=0)
    piece = (piece + swapped(piece, "xh")).astype(jnp.bfloat16)
    sent = jnp.broadcast_to(piece[None], (peers, deep, 128))
    whole = lax.all_to_all(sent, PLANE, 0, 0, tiled=True).reshape(peers * deep, 128)[:rows]
    half = whole.reshape(groups, part, 128).transpose(1, 0, 2).reshape(part, width)
    other = swapped(half, "core")
    out = jnp.where(core == 0, jnp.concatenate([half, other], 0), jnp.concatenate([other, half], 0))
    return out.T


def shards(features, img_weight, text_embed, log_scale, logit_bias):
    logit_scale = jnp.exp(log_scale[0])
    offset_value = logit_bias[0]
    row_count = features.shape[0]
    half_width = img_weight.shape[1]
    img_raw = jnp.dot(features, img_weight, preferred_element_type=jnp.float32)
    txt_raw = text_embed.astype(jnp.float32)
    img_sq, txt_sq = lax.psum(
        (
            jnp.sum(img_raw * img_raw, axis=1, keepdims=True),
            jnp.sum(txt_raw * txt_raw, axis=1, keepdims=True),
        ),
        "rep",
    )
    img_inv = lax.rsqrt(img_sq + epsilon)
    txt_inv = lax.rsqrt(txt_sq + epsilon)
    img_hat = img_raw * img_inv
    txt_hat = txt_raw * txt_inv
    img_bf = img_hat.astype(jnp.bfloat16)
    txt_bf = txt_hat.astype(jnp.bfloat16)
    img_use, text_span = (
        lax.all_gather(img_bf, "rep", axis=1, tiled=True),
        lax.all_gather(txt_bf, "rep", axis=1, tiled=True),
    )
    positives = jnp.eye(row_count, dtype=jnp.float32)
    grad_img = jnp.zeros(img_use.shape, jnp.float32)
    carried = jnp.zeros(text_span.shape, jnp.float32)
    for stride in range(STEPS + 1):
        if stride > 0:
            text_span = passed_along(text_span, 1)
            carried = passed_along(carried.astype(jnp.bfloat16), 1).astype(carried.dtype)
        scores = lax.dot_general(
            img_use, text_span, (((1,), (1,)), ((), ())), preferred_element_type=jnp.float32
        )
        logits = logit_scale * scores + offset_value
        sig_grad = jax.nn.sigmoid(logits)
        if stride == 0:
            sig_grad = sig_grad - positives
        grad_bf = sig_grad.astype(jnp.bfloat16)
        grad_img = grad_img + logit_scale * jnp.dot(
            grad_bf, text_span, preferred_element_type=jnp.float32
        )
        contrib = logit_scale * lax.dot_general(
            grad_bf, img_use, (((0,), (0,)), ((), ())), preferred_element_type=jnp.float32
        )
        carried = carried + contrib
    grad_txt = passed_along(carried.astype(jnp.bfloat16), -STEPS).astype(carried.dtype)
    column_start = lax.axis_index("rep") * half_width
    grad_img = lax.dynamic_slice_in_dim(grad_img, column_start, half_width, 1)
    grad_txt = lax.dynamic_slice_in_dim(grad_txt, column_start, half_width, 1)
    img_dot, txt_dot = lax.psum(
        (
            jnp.sum(img_hat * grad_img, axis=1, keepdims=True),
            jnp.sum(txt_hat * grad_txt, axis=1, keepdims=True),
        ),
        "rep",
    )
    image_grad = ((grad_img - img_hat * img_dot) * img_inv).astype(jnp.bfloat16)
    text_grad = ((grad_txt - txt_hat * txt_dot) * txt_inv).astype(jnp.bfloat16)
    return (image_grad, text_grad, weight_sum(features, image_grad))


def solution(mesh):
    fine = Mesh(mesh.devices.reshape(8, 2, 8, 2, 2), AXES)
    in_specs = (P(DP, None), P(None, "rep"), P(DP, "rep"), P(), P())
    out_specs = (P(DP, "rep"), P(DP, "rep"), P(None, "rep"))
    return jax.shard_map(shards, mesh=fine, in_specs=in_specs, out_specs=out_specs, check_vma=False)
```

```python
import functools

import jax
import jax.numpy as jnp
from jax import lax
from jax.experimental import pallas as pl
from jax.experimental.pallas import tpu as pltpu
from jax.sharding import Mesh, PartitionSpec as P

AXES = ("z", "xh", "y", "core", "rep")
DP = ("z", "xh", "y", "core")
PLANE = ("z", "y")
SIZES = (8, 2, 8, 2, 2)
N_DP, RUN = 256, 16

epsilon = 1e-06
f32, bf16 = jnp.float32, jnp.bfloat16


def shifted(array, by):
    pairs = []
    for block in range(N_DP):
        to = (block + by) % N_DP
        cross = block // RUN != to // RUN
        pairs += [(2 * block + rep, 2 * to + (1 - rep if cross else rep)) for rep in range(2)]
    return lax.ppermute(array, AXES, pairs)


def swapped(array, axis):
    return lax.ppermute(array, axis, [(0, 1), (1, 0)])


def dot(a, b, contract):
    return lax.dot_general(a, b, ((contract[:1], contract[1:]), ((), ())), preferred_element_type=f32)


def pairs_kernel(
    flags, log_scale, bias, t0, tm, p0, p1, i0, ie, if_,
    gi_own, gt_own, gt_back, gi_back, d_p1, d_p0, w_own, w_next,
    ip, i0_n, ip_n,
):
    half = ie.shape[0]
    core, ft, fi = flags[0], flags[1], flags[2]
    scale = jnp.exp(jnp.full((1, 1), log_scale[0], f32))
    offset = bias[0]
    second = core == 1

    def part(which):
        return pl.ds(pl.multiple_of(which * half, half), half)

    ip[part(fi)] = ie[...]
    ip[part(1 - fi)] = if_[...]
    i0_n[...] = i0[...].T
    ip_n[...] = ip[...].T

    def inverse(ref):
        values = ref[...].astype(f32)
        return lax.rsqrt(jnp.sum(values * values, axis=0, keepdims=True) + epsilon)

    def column(row):
        return jnp.broadcast_to(row, (128, row.shape[1])).T[:, :1]

    def row(col):
        return jnp.broadcast_to(col, (col.shape[0], 128)).T[:1]

    i0_inv, ip_inv = inverse(i0), inverse(ip)
    t0_inv, tm_inv, p0_inv, p1_inv = inverse(t0), inverse(tm), inverse(p0), inverse(p1)
    i0_col, ip_col = column(i0_inv), column(ip_inv)

    def pair(image, text, flip, image_col, text_inv, diagonal=False):
        raw = dot(image[:, :half], text[part(flip)], (1, 0)) + dot(image[:, half:], text[part(1 - flip)], (1, 0))
        s = raw * image_col * text_inv
        g = 1.0 / (1.0 + jnp.exp(-(scale * s + offset)))
        if diagonal:
            at = lax.broadcasted_iota(jnp.int32, g.shape, 0) == lax.broadcasted_iota(jnp.int32, g.shape, 1)
            g = g - jnp.where(at, 1.0, 0.0)
        gs = g * s
        return (
            (g * text_inv).astype(bf16),
            (g * image_col).astype(bf16),
            jnp.sum(gs, axis=1, keepdims=True),
            jnp.sum(gs, axis=0, keepdims=True),
        )

    a0, b0, r0, c0 = pair(i0_n, t0, 0, i0_col, t0_inv, True)
    a1, b1, r1, c1 = pair(i0_n, tm, ft, i0_col, tm_inv)
    a2, b2, r2, c2 = pair(ip_n, tm, ft, ip_col, tm_inv)
    a3, b3, r3, c3 = pair(i0_n, p1, ft, i0_col, p1_inv)

    def out_text(grad, text, inv, dots):
        return (grad - text.astype(f32) * (inv * dots)) * (scale * inv)

    def out_image(grad, image, inv, dots):
        return (grad - image.astype(f32) * (inv * dots)) * (scale * inv)

    gt_own[...] = out_text(dot(i0[:half], b0, (1, 0)), t0[:half], t0_inv, c0)
    back = dot(i0[part(ft)], b1, (1, 0)) + dot(ip[part(ft)], b2, (1, 0))
    gt_back[...] = out_text(back, tm[:half], tm_inv, c1 + c2)
    own = (
        dot(t0[:half], a0, (1, 1))
        + dot(tm[part(ft)], a1, (1, 1))
        + dot(p1[part(ft)], a3, (1, 1))
    )
    d3 = dot(i0[part(ft)], b3, (1, 0))

    @pl.when(core == 0)
    def _():
        a4, b4, r4, c4 = pair(ip_n, p1, ft, ip_col, p1_inv)
        whole = out_image(own, i0[:half], i0_inv, row(r0 + r1 + r3))
        gi_own[...] = whole
        w_own[...] = whole.astype(bf16)
        dots = row(r2 + r4)
        first = tm[part(ft)], p1[part(ft)]
        other = tm[part(1 - ft)], p1[part(1 - ft)]
        g_first = out_image(dot(first[0], a2, (1, 1)) + dot(first[1], a4, (1, 1)), ip[:half], ip_inv, dots).astype(bf16)
        w_next[...] = g_first
        gi_back[...] = g_first

        @pl.when(fi == 1)
        def _():
            g_other = dot(other[0], a2, (1, 1)) + dot(other[1], a4, (1, 1))
            gi_back[...] = out_image(g_other, ip[half:], ip_inv, dots).astype(bf16)

        both = d3 + dot(ip[part(ft)], b4, (1, 0))
        d_p1[...] = out_text(both, p1[:half], p1_inv, c3 + c4).astype(bf16)
        d_p0[...] = jnp.zeros(d_p0.shape, bf16)

    @pl.when(second)
    def _():
        a4, b4, r4, c4 = pair(i0_n, p0, 0, i0_col, p0_inv)
        whole = out_image(own + dot(p0[:half], a4, (1, 1)), i0[:half], i0_inv, row(r0 + r1 + r3 + r4))
        gi_own[...] = whole
        w_own[...] = whole.astype(bf16)
        dots = row(r2)
        g_first = out_image(dot(tm[part(ft)], a2, (1, 1)), ip[:half], ip_inv, dots).astype(bf16)
        w_next[...] = g_first
        gi_back[...] = g_first

        @pl.when(fi == 1)
        def _():
            gi_back[...] = out_image(dot(tm[part(1 - ft)], a2, (1, 1)), ip[half:], ip_inv, dots).astype(bf16)

        d_p1[...] = out_text(d3, p1[:half], p1_inv, c3).astype(bf16)
        d_p0[...] = out_text(dot(i0[:half], b4, (1, 0)), p0[:half], p0_inv, c4).astype(bf16)


def block_pairs(flags, log_scale, bias, t0, tm, p0, p1, i0, ie, if_):
    half, rows = ie.shape
    smem, vmem = pl.BlockSpec(memory_space=pltpu.SMEM), pl.BlockSpec(memory_space=pltpu.VMEM)
    out = lambda dtype: jax.ShapeDtypeStruct((half, rows), dtype)
    return pl.pallas_call(
        pairs_kernel,
        out_shape=[out(f32)] * 3 + [out(bf16)] * 5,
        in_specs=[smem] * 3 + [vmem] * 7,
        out_specs=[vmem] * 8,
        scratch_shapes=[
            pltpu.VMEM((2 * half, rows), bf16),
            pltpu.VMEM((rows, 2 * half), bf16),
            pltpu.VMEM((rows, 2 * half), bf16),
        ],
        compiler_params=pltpu.CompilerParams(vmem_limit_bytes=48 * 2**20),
        cost_estimate=pl.CostEstimate(flops=1_700_000_000, bytes_accessed=8_000_000, transcendentals=330_000),
        name="block_pairs",
    )(flags, log_scale, bias, t0, tm, p0, p1, i0, ie, if_)


def weight_kernel(which, w_own, w_next, features, next_features, out):
    part = w_own.shape[0] // 2
    at = pl.ds(pl.multiple_of(which[0] * part, part), part)
    a, b = w_own[at], w_next[at]
    for group in range(features.shape[1] // 128):
        columns = slice(group * 128, group * 128 + 128)
        total = dot(a, features[:, columns], (1, 0)) + dot(b, next_features[:, columns], (1, 0))
        out[group * part : (group + 1) * part] = total.astype(out.dtype)


def weight_part(which, w_own, w_next, features, next_features, dtype):
    part, width = w_own.shape[0] // 2, features.shape[1]
    smem, vmem = pl.BlockSpec(memory_space=pltpu.SMEM), pl.BlockSpec(memory_space=pltpu.VMEM)
    return pl.pallas_call(
        weight_kernel,
        out_shape=jax.ShapeDtypeStruct((part * width // 128, 128), dtype),
        in_specs=[smem] + [vmem] * 4,
        out_specs=vmem,
        compiler_params=pltpu.CompilerParams(vmem_limit_bytes=32 * 2**20),
        cost_estimate=pl.CostEstimate(flops=340_000_000, bytes_accessed=3_000_000, transcendentals=0),
        name="weight_part",
    )(which, w_own, w_next, features, next_features)


def weight_sum(w_own, w_next, features, next_features):
    peers = lax.axis_size(PLANE)
    core = lax.axis_index("core")
    part, width = w_own.shape[0] // 2, features.shape[1]
    groups = width // 128
    rows = groups * part
    index = core.astype(jnp.int32).reshape(1)
    theirs = weight_part(1 - index, w_own, w_next, features, next_features, bf16)
    mine = weight_part(index, w_own, w_next, features, next_features, f32)
    tiles = (mine + swapped(theirs, "core").astype(f32)).astype(bf16)
    deep = -(-rows // (peers * 16)) * 16
    tiles = jnp.pad(tiles, ((0, peers * deep - rows), (0, 0))).reshape(peers, deep, 128)
    pieces = lax.all_to_all(tiles, PLANE, 0, 0, tiled=True)
    piece = jnp.sum(pieces.astype(f32), axis=0)
    piece = (piece + swapped(piece, "xh")).astype(bf16)
    sent = jnp.broadcast_to(piece[None], (peers, deep, 128))
    whole = lax.all_to_all(sent, PLANE, 0, 0, tiled=True).reshape(peers * deep, 128)
    other = swapped(whole, "core")
    first, last = jnp.where(core == 0, whole, other), jnp.where(core == 0, other, whole)
    spread = lambda x: x[:rows].reshape(groups, part, 128).transpose(1, 0, 2).reshape(part, width)
    return jnp.concatenate([spread(first), spread(last)], 0)


def shards(features, img_weight, text_embed, log_scale, logit_bias):
    core, y = lax.axis_index("core"), lax.axis_index("y")
    last = lax.axis_size("y") - 1
    flags = jnp.stack([core, y == 0, y == last]).astype(jnp.int32)
    t_own = text_embed.T
    t_far = swapped(t_own, "rep")
    t_a = shifted(t_own, 2)
    next_features = shifted(features, -2)
    i_own = dot(img_weight, features, (0, 1)).astype(bf16)
    i_far = swapped(i_own, "rep")
    i_e = shifted(i_own, -2)
    t_c = shifted(t_far, 2)
    i_f = shifted(i_far, -2)
    t0 = jnp.concatenate([t_own, t_far], 0)
    tm = jnp.concatenate([t_a, t_c], 0)
    p0 = lax.ppermute(t0, "core", [(0, 1)])
    p1 = swapped(tm, "core")
    i0 = jnp.concatenate([i_own, i_far], 0)
    gi_own, gt_own, gt_back, gi_back, d_p1, d_p0, w_own, w_next = block_pairs(
        flags, log_scale, logit_bias, t0, tm, p0, p1, i0, i_e, i_f
    )
    gi_came = shifted(gi_back, 2)
    d_p1_came = swapped(d_p1, "core")
    d_p0_came = lax.ppermute(d_p0, "core", [(1, 0)])
    gt_came = shifted((gt_back + d_p1_came.astype(f32)).astype(bf16), -2)
    image_grad = (gi_own + gi_came.astype(f32)).astype(bf16)
    text_grad = (gt_own + gt_came.astype(f32) + d_p0_came.astype(f32)).astype(bf16)
    weight_grad = weight_sum(w_own, w_next, features, next_features)
    return image_grad.T, text_grad.T, weight_grad.T


def solution(mesh):
    fine = Mesh(mesh.devices.reshape(SIZES), AXES)
    in_specs = (P(DP, None), P(None, "rep"), P(DP, "rep"), P(), P())
    out_specs = (P(DP, "rep"), P(DP, "rep"), P(None, "rep"))
    return jax.shard_map(shards, mesh=fine, in_specs=in_specs, out_specs=out_specs, check_vma=False)
```

```python
import jax
import jax.numpy as jnp
from jax import lax
from jax.experimental import pallas as pl
from jax.experimental.pallas import tpu as pltpu
from jax.sharding import Mesh, PartitionSpec as P

AXES = ("z", "xh", "y", "core", "rep")
DP = ("z", "xh", "y", "core")
PLANE = ("z", "y")
SIZES = (8, 2, 8, 2, 2)
N_DP, RUN = 256, 16

epsilon = 1e-06
f32, bf16 = jnp.float32, jnp.bfloat16


def shifted(array, by):
    pairs = []
    for block in range(N_DP):
        to = (block + by) % N_DP
        cross = block // RUN != to // RUN
        pairs += [(2 * block + rep, 2 * to + (1 - rep if cross else rep)) for rep in range(2)]
    return lax.ppermute(array, AXES, pairs)


def swapped(array, axis):
    return lax.ppermute(array, axis, [(0, 1), (1, 0)])


def dot(a, b, contract):
    return lax.dot_general(a, b, ((contract[:1], contract[1:]), ((), ())), preferred_element_type=f32)


def pairs_kernel(
    flags, log_scale, bias, t0, tm, p0, p1, i0, came,
    gi_own, gt_own, gt_back, gi_back, d_p1, d_p0, w_own, w_next,
    ip, i0_n, ip_n,
):
    half = came.shape[0] // 2
    core, ft, fi = flags[0], flags[1], flags[2]
    scale = jnp.exp(jnp.full((1, 1), log_scale[0], f32))
    offset = bias[0]
    second = core == 1

    def part(which):
        return pl.ds(pl.multiple_of(which * half, half), half)

    ip[:half] = came[part(fi)]
    ip[half:] = came[part(1 - fi)]
    i0_n[...] = i0[...].T
    ip_n[...] = ip[...].T

    def inverse(ref):
        values = ref[...].astype(f32)
        return lax.rsqrt(jnp.sum(values * values, axis=0, keepdims=True) + epsilon)

    def column(row):
        return jnp.broadcast_to(row, (128, row.shape[1])).T[:, :1]

    def row(col):
        return jnp.broadcast_to(col, (col.shape[0], 128)).T[:1]

    i0_inv, ip_inv = inverse(i0), inverse(ip)
    t0_inv, tm_inv, p0_inv, p1_inv = inverse(t0), inverse(tm), inverse(p0), inverse(p1)
    i0_col, ip_col = column(i0_inv), column(ip_inv)

    def pair(image, text, flip, image_col, text_inv, diagonal=False):
        raw = dot(image[:, :half], text[part(flip)], (1, 0)) + dot(image[:, half:], text[part(1 - flip)], (1, 0))
        s = raw * image_col * text_inv
        g = 1.0 / (1.0 + jnp.exp(-(scale * s + offset)))
        if diagonal:
            at = lax.broadcasted_iota(jnp.int32, g.shape, 0) == lax.broadcasted_iota(jnp.int32, g.shape, 1)
            g = g - jnp.where(at, 1.0, 0.0)
        gs = g * s
        return (
            (g * text_inv).astype(bf16),
            (g * image_col).astype(bf16),
            jnp.sum(gs, axis=1, keepdims=True),
            jnp.sum(gs, axis=0, keepdims=True),
        )

    a0, b0, r0, c0 = pair(i0_n, t0, 0, i0_col, t0_inv, True)
    a1, b1, r1, c1 = pair(i0_n, tm, ft, i0_col, tm_inv)
    a2, b2, r2, c2 = pair(ip_n, tm, ft, ip_col, tm_inv)
    a3, b3, r3, c3 = pair(i0_n, p1, ft, i0_col, p1_inv)

    def out_text(grad, text, inv, dots):
        return (grad - text.astype(f32) * (inv * dots)) * (scale * inv)

    def out_image(grad, image, inv, dots):
        return (grad - image.astype(f32) * (inv * dots)) * (scale * inv)

    gt_own[...] = out_text(dot(i0[:half], b0, (1, 0)), t0[:half], t0_inv, c0)
    back = dot(i0[part(ft)], b1, (1, 0)) + dot(ip[part(ft)], b2, (1, 0))
    gt_back[...] = out_text(back, tm[:half], tm_inv, c1 + c2)
    own = (
        dot(t0[:half], a0, (1, 1))
        + dot(tm[part(ft)], a1, (1, 1))
        + dot(p1[part(ft)], a3, (1, 1))
    )
    d3 = dot(i0[part(ft)], b3, (1, 0))

    @pl.when(core == 0)
    def _():
        a4, b4, r4, c4 = pair(ip_n, p1, ft, ip_col, p1_inv)
        whole = out_image(own, i0[:half], i0_inv, row(r0 + r1 + r3))
        gi_own[...] = whole
        w_own[...] = whole.astype(bf16)
        dots = row(r2 + r4)
        first = tm[part(ft)], p1[part(ft)]
        other = tm[part(1 - ft)], p1[part(1 - ft)]
        g_first = out_image(dot(first[0], a2, (1, 1)) + dot(first[1], a4, (1, 1)), ip[:half], ip_inv, dots).astype(bf16)
        w_next[...] = g_first
        gi_back[...] = g_first

        @pl.when(fi == 1)
        def _():
            g_other = dot(other[0], a2, (1, 1)) + dot(other[1], a4, (1, 1))
            gi_back[...] = out_image(g_other, ip[half:], ip_inv, dots).astype(bf16)

        both = d3 + dot(ip[part(ft)], b4, (1, 0))
        d_p1[...] = out_text(both, p1[:half], p1_inv, c3 + c4).astype(bf16)
        d_p0[...] = jnp.zeros(d_p0.shape, bf16)

    @pl.when(second)
    def _():
        a4, b4, r4, c4 = pair(i0_n, p0, 0, i0_col, p0_inv)
        whole = out_image(own + dot(p0[:half], a4, (1, 1)), i0[:half], i0_inv, row(r0 + r1 + r3 + r4))
        gi_own[...] = whole
        w_own[...] = whole.astype(bf16)
        dots = row(r2)
        g_first = out_image(dot(tm[part(ft)], a2, (1, 1)), ip[:half], ip_inv, dots).astype(bf16)
        w_next[...] = g_first
        gi_back[...] = g_first

        @pl.when(fi == 1)
        def _():
            gi_back[...] = out_image(dot(tm[part(1 - ft)], a2, (1, 1)), ip[half:], ip_inv, dots).astype(bf16)

        d_p1[...] = out_text(d3, p1[:half], p1_inv, c3).astype(bf16)
        d_p0[...] = out_text(dot(i0[:half], b4, (1, 0)), p0[:half], p0_inv, c4).astype(bf16)


def block_pairs(flags, log_scale, bias, t0, tm, p0, p1, i0, came):
    half, rows = came.shape[0] // 2, came.shape[1]
    smem, vmem = pl.BlockSpec(memory_space=pltpu.SMEM), pl.BlockSpec(memory_space=pltpu.VMEM)
    out = lambda dtype: jax.ShapeDtypeStruct((half, rows), dtype)
    return pl.pallas_call(
        pairs_kernel,
        out_shape=[out(f32)] * 3 + [out(bf16)] * 5,
        in_specs=[smem] * 3 + [vmem] * 6,
        out_specs=[vmem] * 8,
        scratch_shapes=[
            pltpu.VMEM((2 * half, rows), bf16),
            pltpu.VMEM((rows, 2 * half), bf16),
            pltpu.VMEM((rows, 2 * half), bf16),
        ],
        compiler_params=pltpu.CompilerParams(vmem_limit_bytes=48 * 2**20),
        cost_estimate=pl.CostEstimate(flops=1_700_000_000, bytes_accessed=8_000_000, transcendentals=330_000),
        name="block_pairs",
    )(flags, log_scale, bias, t0, tm, p0, p1, i0, came)


def weight_kernel(which, w_own, w_next, features, next_features, out):
    part = w_own.shape[0] // 2
    at = pl.ds(pl.multiple_of(which[0] * part, part), part)
    a, b = w_own[at], w_next[at]
    for group in range(features.shape[1] // 128):
        columns = slice(group * 128, group * 128 + 128)
        total = dot(a, features[:, columns], (1, 0)) + dot(b, next_features[:, columns], (1, 0))
        out[group * part : (group + 1) * part] = total.astype(out.dtype)


def weight_part(which, w_own, w_next, features, next_features, dtype):
    part, width = w_own.shape[0] // 2, features.shape[1]
    smem, vmem = pl.BlockSpec(memory_space=pltpu.SMEM), pl.BlockSpec(memory_space=pltpu.VMEM)
    return pl.pallas_call(
        weight_kernel,
        out_shape=jax.ShapeDtypeStruct((part * width // 128, 128), dtype),
        in_specs=[smem] + [vmem] * 4,
        out_specs=vmem,
        compiler_params=pltpu.CompilerParams(vmem_limit_bytes=32 * 2**20),
        cost_estimate=pl.CostEstimate(flops=340_000_000, bytes_accessed=3_000_000, transcendentals=0),
        name="weight_part",
    )(which, w_own, w_next, features, next_features)


def join_kernel(core, mine, other, out):
    part = out.shape[0] // 2
    here = pl.ds(pl.multiple_of(core[0] * part, part), part)
    there = pl.ds(pl.multiple_of((1 - core[0]) * part, part), part)
    for group in range(out.shape[1] // 128):
        rows, columns = slice(group * part, (group + 1) * part), slice(group * 128, group * 128 + 128)
        out[here, columns] = mine[rows]
        out[there, columns] = other[rows]


def joined(core, mine, other, shape):
    smem, vmem = pl.BlockSpec(memory_space=pltpu.SMEM), pl.BlockSpec(memory_space=pltpu.VMEM)
    return pl.pallas_call(
        join_kernel,
        out_shape=jax.ShapeDtypeStruct(shape, bf16),
        in_specs=[smem] + [vmem] * 2,
        out_specs=vmem,
        compiler_params=pltpu.CompilerParams(vmem_limit_bytes=16 * 2**20),
        cost_estimate=pl.CostEstimate(flops=0, bytes_accessed=3_000_000, transcendentals=0),
        name="joined",
    )(core, mine, other)


def shards(features, img_weight, text_embed, log_scale, logit_bias):
    core, y = lax.axis_index("core").astype(jnp.int32), lax.axis_index("y")
    last = lax.axis_size("y") - 1
    flags = jnp.stack([core, y == 0, y == last]).astype(jnp.int32)
    half, width = img_weight.shape[1], features.shape[1]

    t_own = text_embed.T
    t_far = swapped(t_own, "rep")
    next_features = shifted(features, -2)
    i_own = lax.optimization_barrier(dot(img_weight, features, (0, 1)).astype(bf16))
    i_far = swapped(i_own, "rep")
    t0 = jnp.concatenate([t_own, t_far], 0)
    tm = shifted(t0, 2)
    i0 = jnp.concatenate([i_own, i_far], 0)
    i0, next_features = lax.optimization_barrier((i0, next_features))
    ip = shifted(i0, -2)
    p0 = lax.ppermute(t0, "core", [(0, 1)])
    p1 = swapped(tm, "core")
    gi_own, gt_own, gt_back, gi_back, d_p1, d_p0, w_own, w_next = block_pairs(
        flags, log_scale, logit_bias, t0, tm, p0, p1, i0, ip
    )

    index = core.reshape(1)
    theirs = weight_part(1 - index, w_own, w_next, features, next_features, bf16)
    mine = weight_part(index, w_own, w_next, features, next_features, f32)
    peers = lax.axis_size(PLANE)
    rows = mine.shape[0]
    deep = -(-rows // (peers * 16)) * 16
    tiles = (mine + swapped(theirs, "core").astype(f32)).astype(bf16)
    tiles = jnp.pad(tiles, ((0, peers * deep - rows), (0, 0))).reshape(peers, deep, 128)
    pieces = lax.all_to_all(tiles, PLANE, 0, 0, tiled=True)
    gi_came = shifted(gi_back, 2)
    image_grad = (gi_own + gi_came.astype(f32)).astype(bf16)
    gt_sum = (gt_back + swapped(d_p1, "core").astype(f32)).astype(bf16)
    gt_own = gt_own + lax.ppermute(d_p0, "core", [(1, 0)]).astype(f32)
    piece = jnp.sum(pieces.astype(f32), axis=0)
    piece = (piece + swapped(piece, "xh")).astype(bf16)
    piece, image_grad, gt_sum, gt_own = lax.optimization_barrier((piece, image_grad, gt_sum, gt_own))
    sent = jnp.broadcast_to(piece[None], (peers, deep, 128))
    whole = lax.all_to_all(sent, PLANE, 0, 0, tiled=True).reshape(peers * deep, 128)
    text_grad = (gt_own + shifted(gt_sum, -2).astype(f32)).astype(bf16)
    whole, text_grad = lax.optimization_barrier((whole, text_grad))
    weight_grad = joined(index, whole, swapped(whole, "core"), (half, width))
    return image_grad.T, text_grad.T, weight_grad.T


def solution(mesh):
    fine = Mesh(mesh.devices.reshape(SIZES), AXES)
    in_specs = (P(DP, None), P(None, "rep"), P(DP, "rep"), P(), P())
    out_specs = (P(DP, "rep"), P(DP, "rep"), P(None, "rep"))
    return jax.shard_map(shards, mesh=fine, in_specs=in_specs, out_specs=out_specs, check_vma=False)
```

```python
import functools

import jax
import jax.numpy as jnp
from jax import lax
from jax.experimental import pallas as pl
from jax.experimental.pallas import tpu as pltpu
from jax.sharding import Mesh, PartitionSpec as P

AXES = ("z", "xh", "y", "core", "rep")
DP = ("z", "xh", "y", "core")
PLANE = ("z", "y")
SIZES = (8, 2, 8, 2, 2)
N_DP, RUN = 256, 16

epsilon = 1e-06
f32, bf16 = jnp.float32, jnp.bfloat16


def shifted(array, by):
    pairs = []
    for block in range(N_DP):
        to = (block + by) % N_DP
        cross = block // RUN != to // RUN
        pairs += [(2 * block + rep, 2 * to + (1 - rep if cross else rep)) for rep in range(2)]
    return lax.ppermute(array, AXES, pairs)


def swapped(array, axis):
    return lax.ppermute(array, axis, [(0, 1), (1, 0)])


def dot(a, b, contract):
    return lax.dot_general(a, b, ((contract[:1], contract[1:]), ((), ())), preferred_element_type=f32)


def column(row):
    return jnp.broadcast_to(row, (128, row.shape[1])).T[:, :1]


def row(col):
    return jnp.broadcast_to(col, (col.shape[0], 128)).T[:1]


def inverse(*refs):
    squares = 0.0
    for ref in refs:
        values = ref[...].astype(f32)
        squares = squares + jnp.sum(values * values, axis=0, keepdims=True)
    return lax.rsqrt(squares + epsilon)


def part(which, size):
    return pl.ds(pl.multiple_of(which * size, size), size)


def pair(scale, offset, image, text, flip, image_col, text_inv, diagonal=False):
    half = text.shape[0] // 2
    raw = dot(image[:, :half], text[part(flip, half)], (1, 0)) + dot(image[:, half:], text[part(1 - flip, half)], (1, 0))
    s = raw * image_col * text_inv
    g = 1.0 / (1.0 + jnp.exp(-(scale * s + offset)))
    if diagonal:
        at = lax.broadcasted_iota(jnp.int32, g.shape, 0) == lax.broadcasted_iota(jnp.int32, g.shape, 1)
        g = g - jnp.where(at, 1.0, 0.0)
    gs = g * s
    return (
        (g * text_inv).astype(bf16),
        (g * image_col).astype(bf16),
        jnp.sum(gs, axis=1, keepdims=True),
        jnp.sum(gs, axis=0, keepdims=True),
    )


def removed(grad, hat, scale, inv, dots):
    return (grad - hat.astype(f32) * (inv * dots)) * (scale * inv)


def place():
    y = lax.axis_index("y")
    return lax.axis_index("core"), (y == 0).astype(jnp.int32), (y == lax.axis_size("y") - 1).astype(jnp.int32)


I0_INV, T0_INV, TM_INV, DOT01, C0, C1 = range(6)
IP_INV, P1_INV, P0_INV, C2, C3, C4 = range(6)


def first_kernel(log_scale, bias, t0, tm, i_own, i_far, own, i0_n, b, stats):
    half, (_, ft, _) = own.shape[0], place()
    scale, offset = jnp.exp(jnp.full((1, 1), log_scale[0], f32)), bias[0]
    i0_n[:, :half] = i_own[...].T
    i0_n[:, half:] = i_far[...].T
    i0_inv, t0_inv, tm_inv = inverse(i_own, i_far), inverse(t0), inverse(tm)
    i0_col = column(i0_inv)
    a0, b[0], r0, c0 = pair(scale, offset, i0_n, t0, 0, i0_col, t0_inv, True)
    a1, b[1], r1, c1 = pair(scale, offset, i0_n, tm, ft, i0_col, tm_inv)
    own[...] = dot(t0[:half], a0, (1, 1)) + dot(tm[part(ft, half)], a1, (1, 1))
    stats[...] = jnp.concatenate([i0_inv, t0_inv, tm_inv, row(r0 + r1), c0, c1, c0, c1], 0)


def second_kernel(
    log_scale, bias, tm, p0, p1, i_e, i_f, own, i_own, i0_n, stats,
    gi_own, gi_back, w_own, w_next, ip, b, stats2,
    ip_n,
):
    half = own.shape[0]
    core, ft, fi = place()
    scale, offset = jnp.exp(jnp.full((1, 1), log_scale[0], f32)), bias[0]
    ip[part(fi, half)] = i_e[...]
    ip[part(1 - fi, half)] = i_f[...]
    ip_n[...] = ip[...].T
    i0_inv, tm_inv, dots01 = stats[I0_INV : I0_INV + 1], stats[TM_INV : TM_INV + 1], stats[DOT01 : DOT01 + 1]
    ip_inv, p1_inv, p0_inv = inverse(ip), inverse(p1), inverse(p0)
    i0_col, ip_col = column(i0_inv), column(ip_inv)
    a2, b[0], r2, c2 = pair(scale, offset, ip_n, tm, ft, ip_col, tm_inv)
    a3, b[1], r3, c3 = pair(scale, offset, i0_n, p1, ft, i0_col, p1_inv)
    own_sum = own[...] + dot(p1[part(ft, half)], a3, (1, 1))

    def store_next(first, other, dots):
        near = removed(first(), ip[:half], scale, ip_inv, dots).astype(bf16)
        gi_back[...] = near
        w_next[...] = near

        @pl.when(fi == 1)
        def _():
            gi_back[...] = removed(other(), ip[half:], scale, ip_inv, dots).astype(bf16)

    def store_stats(c4):
        stats2[...] = jnp.concatenate([ip_inv, p1_inv, p0_inv, c2, c3, c4, c2, c3], 0)

    @pl.when(core == 0)
    def _():
        a4, b[2], r4, c4 = pair(scale, offset, ip_n, p1, ft, ip_col, p1_inv)
        whole = removed(own_sum, i_own[...], scale, i0_inv, dots01 + row(r3))
        gi_own[...] = whole
        w_own[...] = whole.astype(bf16)
        store_next(
            lambda: dot(tm[part(ft, half)], a2, (1, 1)) + dot(p1[part(ft, half)], a4, (1, 1)),
            lambda: dot(tm[part(1 - ft, half)], a2, (1, 1)) + dot(p1[part(1 - ft, half)], a4, (1, 1)),
            row(r2 + r4),
        )
        store_stats(c4)

    @pl.when(core == 1)
    def _():
        a4, b[2], r4, c4 = pair(scale, offset, i0_n, p0, 0, i0_col, p0_inv)
        whole = removed(own_sum + dot(p0[:half], a4, (1, 1)), i_own[...], scale, i0_inv, dots01 + row(r3 + r4))
        gi_own[...] = whole
        w_own[...] = whole.astype(bf16)
        store_next(
            lambda: dot(tm[part(ft, half)], a2, (1, 1)),
            lambda: dot(tm[part(1 - ft, half)], a2, (1, 1)),
            row(r2),
        )
        store_stats(c4)


def text_kernel(log_scale, t0, tm, p0, p1, i_own, i_far, ip, b01, b234, stats, stats2, gt_own, gt_back, d_p1, d_p0):
    half = gt_own.shape[0]
    core, ft, _ = place()
    scale = jnp.exp(jnp.full((1, 1), log_scale[0], f32))
    t0_inv, tm_inv, p1_inv = stats[T0_INV : T0_INV + 1], stats[TM_INV : TM_INV + 1], stats2[P1_INV : P1_INV + 1]
    c0, c1, c2, c3, c4 = stats[C0 : C0 + 1], stats[C1 : C1 + 1], stats2[C2 : C2 + 1], stats2[C3 : C3 + 1], stats2[C4 : C4 + 1]
    gt_own[...] = removed(dot(i_own[...], b01[0], (1, 0)), t0[:half], scale, t0_inv, c0)
    own, next_ = jnp.where(ft == 1, i_far[...], i_own[...]), ip[part(ft, half)]
    back = dot(own, b01[1], (1, 0)) + dot(next_, b234[0], (1, 0))
    gt_back[...] = removed(back, tm[:half], scale, tm_inv, c1 + c2)
    d3 = dot(own, b234[1], (1, 0))

    @pl.when(core == 0)
    def _():
        both = d3 + dot(next_, b234[2], (1, 0))
        d_p1[...] = removed(both, p1[:half], scale, p1_inv, c3 + c4).astype(bf16)
        d_p0[...] = jnp.zeros(d_p0.shape, bf16)

    @pl.when(core == 1)
    def _():
        d_p1[...] = removed(d3, p1[:half], scale, p1_inv, c3).astype(bf16)
        d_p0[...] = removed(dot(i_own[...], b234[2], (1, 0)), p0[:half], scale, stats2[P0_INV : P0_INV + 1], c4).astype(bf16)


def local(kernel, scalars, args, outs, scratch, flops, name, limit=16):
    smem, vmem = pl.BlockSpec(memory_space=pltpu.SMEM), pl.BlockSpec(memory_space=pltpu.VMEM)
    return pl.pallas_call(
        kernel,
        out_shape=[jax.ShapeDtypeStruct(*out) for out in outs],
        in_specs=[smem] * scalars + [vmem] * (len(args) - scalars),
        out_specs=[vmem] * len(outs),
        scratch_shapes=[pltpu.VMEM(*shape) for shape in scratch],
        compiler_params=pltpu.CompilerParams(vmem_limit_bytes=limit * 2**20),
        cost_estimate=pl.CostEstimate(flops=flops, bytes_accessed=4_000_000, transcendentals=200_000),
        name=name,
    )(*args)


def weight_kernel(other, w_own, w_next, features, next_features, out):
    core, part = lax.axis_index("core"), w_own.shape[0] // 2
    at = pl.ds(pl.multiple_of((1 - core if other else core) * part, part), part)
    a, b = w_own[at], w_next[at]
    for group in range(features.shape[1] // 128):
        columns = slice(group * 128, group * 128 + 128)
        total = dot(a, features[:, columns], (1, 0)) + dot(b, next_features[:, columns], (1, 0))
        out[group * part : (group + 1) * part] = total.astype(out.dtype)
    filled = features.shape[1] // 128 * part
    out[filled:] = jnp.zeros((out.shape[0] - filled, 128), out.dtype)


def join_kernel(mine, other, out):
    core, part = lax.axis_index("core"), out.shape[0] // 2
    here = pl.ds(pl.multiple_of(core * part, part), part)
    there = pl.ds(pl.multiple_of((1 - core) * part, part), part)
    for group in range(out.shape[1] // 128):
        rows, columns = slice(group * part, (group + 1) * part), slice(group * 128, group * 128 + 128)
        out[here, columns] = mine[rows]
        out[there, columns] = other[rows]


def shards(features, img_weight, text_embed, log_scale, logit_bias):
    half, width = img_weight.shape[1], features.shape[1]
    count = features.shape[0]

    t_own = text_embed.T
    t_far = swapped(t_own, "rep")
    t_a = shifted(t_own, 2)
    i_own = lax.optimization_barrier(dot(img_weight, features, (0, 1)).astype(bf16))
    i_far = swapped(i_own, "rep")
    i_e = shifted(i_own, -2)
    t_b = swapped(lax.optimization_barrier((t_a, i_far))[0], "rep")
    next_features = shifted(lax.optimization_barrier((features, t_a))[0], -2)
    i_f = swapped(i_e, "rep")
    t0 = jnp.concatenate([t_own, t_far], 0)
    tm = jnp.concatenate([t_a, t_b], 0)
    late_tm, i_f, next_features = lax.optimization_barrier((tm, i_f, next_features))
    p1 = swapped(late_tm, "core")
    p0 = lax.ppermute(t0, "core", [(0, 1)])
    whole, square, by_row = (half, count), (count, count), (8, count)
    own, i0_n, b01, stats = local(
        first_kernel, 2, (log_scale, logit_bias, t0, tm, i_own, i_far),
        [(whole, f32), ((count, 2 * half), bf16), ((2, *square), bf16), (by_row, f32)], [], 500_000_000, "first_pairs",
    )
    gi_own, gi_back, w_own, w_next, ip, b234, stats2 = local(
        second_kernel, 2, (log_scale, logit_bias, tm, p0, p1, i_e, i_f, own, i_own, i0_n, stats),
        [(whole, f32), (whole, bf16), (whole, bf16), (whole, bf16), ((2 * half, count), bf16), ((3, *square), bf16), (by_row, f32)],
        [((count, 2 * half), bf16)], 800_000_000, "second_pairs",
    )
    gt_own, gt_back, d_p1, d_p0 = local(
        text_kernel, 1, (log_scale, t0, tm, p0, p1, i_own, i_far, ip, b01, b234, stats, stats2),
        [(whole, f32), (whole, f32), (whole, bf16), (whole, bf16)], [], 400_000_000, "text_gradients",
    )

    peers = lax.axis_size(PLANE)
    deep = -(-half * width // (2 * 128 * peers * 16)) * 16
    theirs, mine = (
        local(
            functools.partial(weight_kernel, other), 0, (w_own, w_next, features, next_features),
            [((peers * deep, 128), dtype)], [], 340_000_000, "weight_part", 8,
        )[0]
        for other, dtype in ((True, bf16), (False, f32))
    )
    tiles = (mine + swapped(theirs, "core").astype(f32)).astype(bf16).reshape(peers, deep, 128)
    pieces = lax.all_to_all(tiles, PLANE, 0, 0, tiled=True)
    gi_came = shifted(gi_back, 2)
    gt_sum = (gt_back + swapped(d_p1, "core").astype(f32)).astype(bf16)
    d_p0_came = lax.ppermute(d_p0, "core", [(1, 0)])
    gt_came = shifted(gt_sum, -2)
    piece = jnp.sum(pieces.astype(f32), axis=0)
    piece = (piece + swapped(piece, "xh")).astype(bf16)
    piece, gi_came, gt_came, d_p0_came = lax.optimization_barrier((piece, gi_came, gt_came, d_p0_came))
    sent = jnp.broadcast_to(piece[None], (peers, deep, 128))
    whole = lax.all_to_all(sent, PLANE, 0, 0, tiled=True).reshape(peers * deep, 128)
    image_grad = (gi_own + gi_came.astype(f32)).astype(bf16)
    text_grad = (gt_own + gt_came.astype(f32) + d_p0_came.astype(f32)).astype(bf16)
    whole, image_grad, text_grad = lax.optimization_barrier((whole, image_grad, text_grad))
    (weight_grad,) = local(join_kernel, 0, (whole, swapped(whole, "core")), [((half, width), bf16)], [], 0, "joined", 4)
    return image_grad.T, text_grad.T, weight_grad.T


def solution(mesh):
    fine = Mesh(mesh.devices.reshape(SIZES), AXES)
    in_specs = (P(DP, None), P(None, "rep"), P(DP, "rep"), P(), P())
    out_specs = (P(DP, "rep"), P(DP, "rep"), P(None, "rep"))
    return jax.shard_map(shards, mesh=fine, in_specs=in_specs, out_specs=out_specs, check_vma=False)
```

```python
import functools

import jax
import jax.numpy as jnp
from jax import lax
from jax.experimental import pallas as pl
from jax.experimental.pallas import tpu as pltpu
from jax.sharding import Mesh, PartitionSpec as P

AXES = ("z", "xh", "y", "core", "rep")
DP = ("z", "xh", "y", "core")
PLANE = ("z", "y")
SIZES = (8, 2, 8, 2, 2)
N_DP, RUN = 256, 16

epsilon = 1e-06
f32, bf16 = jnp.float32, jnp.bfloat16


def shifted(array, by):
    pairs = []
    for block in range(N_DP):
        to = (block + by) % N_DP
        cross = block // RUN != to // RUN
        pairs += [(2 * block + rep, 2 * to + (1 - rep if cross else rep)) for rep in range(2)]
    return lax.ppermute(array, AXES, pairs)


def swapped(array, axis):
    return lax.ppermute(array, axis, [(0, 1), (1, 0)])


def dot(a, b, contract):
    return lax.dot_general(a, b, ((contract[:1], contract[1:]), ((), ())), preferred_element_type=f32)


def column(row):
    return jnp.broadcast_to(row, (128, row.shape[1])).T[:, :1]


def row(col):
    return jnp.broadcast_to(col, (col.shape[0], 128)).T[:1]


def inverse(*refs):
    squares = 0.0
    for ref in refs:
        values = ref[...].astype(f32)
        squares = squares + jnp.sum(values * values, axis=0, keepdims=True)
    return lax.rsqrt(squares + epsilon)


def part(which, size):
    return pl.ds(pl.multiple_of(which * size, size), size)


def pair(scale, offset, image, text, flip, image_col, text_inv, diagonal=False):
    half = text.shape[0] // 2
    raw = dot(image[:, :half], text[part(flip, half)], (1, 0)) + dot(image[:, half:], text[part(1 - flip, half)], (1, 0))
    s = raw * image_col * text_inv
    g = 1.0 / (1.0 + jnp.exp(-(scale * s + offset)))
    if diagonal:
        at = lax.broadcasted_iota(jnp.int32, g.shape, 0) == lax.broadcasted_iota(jnp.int32, g.shape, 1)
        g = g - jnp.where(at, 1.0, 0.0)
    gs = g * s
    return (
        (g * text_inv).astype(bf16),
        (g * image_col).astype(bf16),
        jnp.sum(gs, axis=1, keepdims=True),
        jnp.sum(gs, axis=0, keepdims=True),
    )


def removed(grad, hat, scale, inv, dots):
    return (grad - hat.astype(f32) * (inv * dots)) * (scale * inv)


def place():
    y = lax.axis_index("y")
    return lax.axis_index("core"), (y == 0).astype(jnp.int32), (y == lax.axis_size("y") - 1).astype(jnp.int32)


I0_INV, T0_INV, TM_INV, DOT01, C0, C1 = range(6)
IP_INV, P1_INV, P0_INV, C2, C3, C4 = range(6)


def first_kernel(log_scale, bias, t0, tm, i_own, i_far, own, i0_n, b, stats):
    half, (_, ft, _) = own.shape[0], place()
    scale, offset = jnp.exp(jnp.full((1, 1), log_scale[0], f32)), bias[0]
    i0_n[:, :half] = i_own[...].T
    i0_n[:, half:] = i_far[...].T
    i0_inv, t0_inv, tm_inv = inverse(i_own, i_far), inverse(t0), inverse(tm)
    i0_col = column(i0_inv)
    a0, b[0], r0, c0 = pair(scale, offset, i0_n, t0, 0, i0_col, t0_inv, True)
    a1, b[1], r1, c1 = pair(scale, offset, i0_n, tm, ft, i0_col, tm_inv)
    own[...] = dot(t0[:half], a0, (1, 1)) + dot(tm[part(ft, half)], a1, (1, 1))
    stats[...] = jnp.concatenate([i0_inv, t0_inv, tm_inv, row(r0 + r1), c0, c1, c0, c1], 0)


def second_kernel(
    log_scale, bias, tm, p0, p1, i_e, i_f, own, i_own, i0_n, stats,
    gi_own, gi_back, w_own, w_next, b, stats2,
    ip, ip_n,
):
    half = own.shape[0]
    core, ft, fi = place()
    scale, offset = jnp.exp(jnp.full((1, 1), log_scale[0], f32)), bias[0]
    ip[part(fi, half)] = i_e[...]
    ip[part(1 - fi, half)] = i_f[...]
    ip_n[...] = ip[...].T
    i0_inv, tm_inv, dots01 = stats[I0_INV : I0_INV + 1], stats[TM_INV : TM_INV + 1], stats[DOT01 : DOT01 + 1]
    ip_inv, p1_inv, p0_inv = inverse(ip), inverse(p1), inverse(p0)
    i0_col, ip_col = column(i0_inv), column(ip_inv)
    a2, b[0], r2, c2 = pair(scale, offset, ip_n, tm, ft, ip_col, tm_inv)
    a3, b[1], r3, c3 = pair(scale, offset, i0_n, p1, ft, i0_col, p1_inv)
    own_sum = own[...] + dot(p1[part(ft, half)], a3, (1, 1))

    def store_next(first, other, dots):
        near = removed(first(), ip[:half], scale, ip_inv, dots).astype(bf16)
        gi_back[...] = near
        w_next[...] = near

        @pl.when(fi == 1)
        def _():
            gi_back[...] = removed(other(), ip[half:], scale, ip_inv, dots).astype(bf16)

    def store_stats(c4):
        stats2[...] = jnp.concatenate([ip_inv, p1_inv, p0_inv, c2, c3, c4, c2, c3], 0)

    @pl.when(core == 0)
    def _():
        a4, b[2], r4, c4 = pair(scale, offset, ip_n, p1, ft, ip_col, p1_inv)
        whole = removed(own_sum, i_own[...], scale, i0_inv, dots01 + row(r3))
        gi_own[...] = whole
        w_own[...] = whole.astype(bf16)
        store_next(
            lambda: dot(tm[part(ft, half)], a2, (1, 1)) + dot(p1[part(ft, half)], a4, (1, 1)),
            lambda: dot(tm[part(1 - ft, half)], a2, (1, 1)) + dot(p1[part(1 - ft, half)], a4, (1, 1)),
            row(r2 + r4),
        )
        store_stats(c4)

    @pl.when(core == 1)
    def _():
        a4, b[2], r4, c4 = pair(scale, offset, i0_n, p0, 0, i0_col, p0_inv)
        whole = removed(own_sum + dot(p0[:half], a4, (1, 1)), i_own[...], scale, i0_inv, dots01 + row(r3 + r4))
        gi_own[...] = whole
        w_own[...] = whole.astype(bf16)
        store_next(
            lambda: dot(tm[part(ft, half)], a2, (1, 1)),
            lambda: dot(tm[part(1 - ft, half)], a2, (1, 1)),
            row(r2),
        )
        store_stats(c4)


def text_kernel(log_scale, t0, tm, p0, p1, i_own, i_far, i_e, i_f, b01, b234, stats, stats2, gt_own, gt_back, d_p1, d_p0):
    half = gt_own.shape[0]
    core, ft, fi = place()
    scale = jnp.exp(jnp.full((1, 1), log_scale[0], f32))
    t0_inv, tm_inv, p1_inv = stats[T0_INV : T0_INV + 1], stats[TM_INV : TM_INV + 1], stats2[P1_INV : P1_INV + 1]
    c0, c1, c2, c3, c4 = stats[C0 : C0 + 1], stats[C1 : C1 + 1], stats2[C2 : C2 + 1], stats2[C3 : C3 + 1], stats2[C4 : C4 + 1]
    gt_own[...] = removed(dot(i_own[...], b01[0], (1, 0)), t0[:half], scale, t0_inv, c0)
    own = jnp.where(ft == 1, i_far[...], i_own[...])
    next_ = jnp.where(ft == fi, i_e[...], i_f[...])
    back = dot(own, b01[1], (1, 0)) + dot(next_, b234[0], (1, 0))
    gt_back[...] = removed(back, tm[:half], scale, tm_inv, c1 + c2)
    d3 = dot(own, b234[1], (1, 0))

    @pl.when(core == 0)
    def _():
        both = d3 + dot(next_, b234[2], (1, 0))
        d_p1[...] = removed(both, p1[:half], scale, p1_inv, c3 + c4).astype(bf16)
        d_p0[...] = jnp.zeros(d_p0.shape, bf16)

    @pl.when(core == 1)
    def _():
        d_p1[...] = removed(d3, p1[:half], scale, p1_inv, c3).astype(bf16)
        d_p0[...] = removed(dot(i_own[...], b234[2], (1, 0)), p0[:half], scale, stats2[P0_INV : P0_INV + 1], c4).astype(bf16)


def local(kernel, scalars, args, outs, scratch, flops, name, limit=16):
    smem, vmem = pl.BlockSpec(memory_space=pltpu.SMEM), pl.BlockSpec(memory_space=pltpu.VMEM)
    return pl.pallas_call(
        kernel,
        out_shape=[jax.ShapeDtypeStruct(*out) for out in outs],
        in_specs=[smem] * scalars + [vmem] * (len(args) - scalars),
        out_specs=[vmem] * len(outs),
        scratch_shapes=[pltpu.VMEM(*shape) for shape in scratch],
        compiler_params=pltpu.CompilerParams(vmem_limit_bytes=limit * 2**20),
        cost_estimate=pl.CostEstimate(flops=flops, bytes_accessed=4_000_000, transcendentals=200_000),
        name=name,
    )(*args)


def weight_kernel(other, w_own, w_next, features, next_features, out):
    core, part = lax.axis_index("core"), w_own.shape[0] // 2
    at = pl.ds(pl.multiple_of((1 - core if other else core) * part, part), part)
    a, b = w_own[at], w_next[at]
    for group in range(features.shape[1] // 128):
        columns = slice(group * 128, group * 128 + 128)
        total = dot(a, features[:, columns], (1, 0)) + dot(b, next_features[:, columns], (1, 0))
        out[group * part : (group + 1) * part] = total.astype(out.dtype)
    filled = features.shape[1] // 128 * part
    out[filled:] = jnp.zeros((out.shape[0] - filled, 128), out.dtype)


def join_kernel(mine, other, out):
    core, part = lax.axis_index("core"), out.shape[0] // 2
    here = pl.ds(pl.multiple_of(core * part, part), part)
    there = pl.ds(pl.multiple_of((1 - core) * part, part), part)
    for group in range(out.shape[1] // 128):
        rows, columns = slice(group * part, (group + 1) * part), slice(group * 128, group * 128 + 128)
        out[here, columns] = mine[rows]
        out[there, columns] = other[rows]


def shards(features, img_weight, text_embed, log_scale, logit_bias):
    half, width = img_weight.shape[1], features.shape[1]
    count = features.shape[0]

    t_own = text_embed.T
    t_far = swapped(t_own, "rep")
    t_a = shifted(t_own, 2)
    i_own = lax.optimization_barrier(dot(img_weight, features, (0, 1)).astype(bf16))
    i_far = swapped(i_own, "rep")
    i_e = shifted(i_own, -2)
    t_b = swapped(lax.optimization_barrier((t_a, i_far))[0], "rep")
    next_features = shifted(lax.optimization_barrier((features, t_a))[0], -2)
    i_f = swapped(i_e, "rep")
    t0 = jnp.concatenate([t_own, t_far], 0)
    tm = jnp.concatenate([t_a, t_b], 0)
    whole, square, by_row = (half, count), (count, count), (8, count)
    own, i0_n, b01, stats = local(
        first_kernel, 2, (log_scale, logit_bias, t0, tm, i_own, i_far),
        [(whole, f32), ((count, 2 * half), bf16), ((2, *square), bf16), (by_row, f32)], [], 500_000_000, "first_pairs",
    )
    late_tm, i_f, next_features, own = lax.optimization_barrier((tm, i_f, next_features, own))
    p1 = swapped(late_tm, "core")
    p0 = lax.ppermute(t0, "core", [(0, 1)])
    gi_own, gi_back, w_own, w_next, b234, stats2 = local(
        second_kernel, 2, (log_scale, logit_bias, tm, p0, p1, i_e, i_f, own, i_own, i0_n, stats),
        [(whole, f32), (whole, bf16), (whole, bf16), (whole, bf16), ((3, *square), bf16), (by_row, f32)],
        [((2 * half, count), bf16), ((count, 2 * half), bf16)], 800_000_000, "second_pairs",
    )
    gt_own, gt_back, d_p1, d_p0 = local(
        text_kernel, 1, (log_scale, t0, tm, p0, p1, i_own, i_far, i_e, i_f, b01, b234, stats, stats2),
        [(whole, f32), (whole, f32), (whole, bf16), (whole, bf16)], [], 400_000_000, "text_gradients",
    )

    peers = lax.axis_size(PLANE)
    deep = -(-half * width // (2 * 128 * peers * 16)) * 16
    theirs, mine = (
        local(
            functools.partial(weight_kernel, other), 0, (w_own, w_next, features, next_features),
            [((peers * deep, 128), dtype)], [], 340_000_000, "weight_part", 8,
        )[0]
        for other, dtype in ((True, bf16), (False, f32))
    )
    tiles = (mine + swapped(theirs, "core").astype(f32)).astype(bf16).reshape(peers, deep, 128)
    pieces = lax.all_to_all(tiles, PLANE, 0, 0, tiled=True)
    gi_came = shifted(gi_back, 2)
    gt_sum = (gt_back + swapped(d_p1, "core").astype(f32)).astype(bf16)
    d_p0_came = lax.ppermute(d_p0, "core", [(1, 0)])
    gt_came = shifted(gt_sum, -2)
    piece = jnp.sum(pieces.astype(f32), axis=0)
    piece = (piece + swapped(piece, "xh")).astype(bf16)
    piece, gi_came, gt_came, d_p0_came = lax.optimization_barrier((piece, gi_came, gt_came, d_p0_came))
    sent = jnp.broadcast_to(piece[None], (peers, deep, 128))
    whole = lax.all_to_all(sent, PLANE, 0, 0, tiled=True).reshape(peers * deep, 128)
    image_grad = (gi_own + gi_came.astype(f32)).astype(bf16)
    text_grad = (gt_own + gt_came.astype(f32) + d_p0_came.astype(f32)).astype(bf16)
    whole, image_grad, text_grad = lax.optimization_barrier((whole, image_grad, text_grad))
    (weight_grad,) = local(join_kernel, 0, (whole, swapped(whole, "core")), [((half, width), bf16)], [], 0, "joined", 4)
    return image_grad.T, text_grad.T, weight_grad.T


def solution(mesh):
    fine = Mesh(mesh.devices.reshape(SIZES), AXES)
    in_specs = (P(DP, None), P(None, "rep"), P(DP, "rep"), P(), P())
    out_specs = (P(DP, "rep"), P(DP, "rep"), P(None, "rep"))
    return jax.shard_map(shards, mesh=fine, in_specs=in_specs, out_specs=out_specs, check_vma=False)
```

```python
import functools

import jax
import jax.numpy as jnp
from jax import lax
from jax.experimental import pallas as pl
from jax.experimental.pallas import tpu as pltpu
from jax.sharding import Mesh, PartitionSpec as P

AXES = ("z", "xh", "y", "core", "rep")
DP = ("z", "xh", "y", "core")
PLANE = ("z", "y")
SIZES = (8, 2, 8, 2, 2)
N_DP, RUN = 256, 16

epsilon = 1e-06
f32, bf16 = jnp.float32, jnp.bfloat16


def shifted(array, by):
    pairs = []
    for block in range(N_DP):
        to = (block + by) % N_DP
        cross = block // RUN != to // RUN
        pairs += [(2 * block + rep, 2 * to + (1 - rep if cross else rep)) for rep in range(2)]
    return lax.ppermute(array, AXES, pairs)


def swapped(array, axis):
    return lax.ppermute(array, axis, [(0, 1), (1, 0)])


def dot(a, b, contract):
    return lax.dot_general(a, b, ((contract[:1], contract[1:]), ((), ())), preferred_element_type=f32)


def column(row):
    return jnp.broadcast_to(row, (128, row.shape[1])).T[:, :1]


def row(col):
    return jnp.broadcast_to(col, (col.shape[0], 128)).T[:1]


def inverse(*refs):
    squares = 0.0
    for ref in refs:
        values = ref[...].astype(f32)
        squares = squares + jnp.sum(values * values, axis=0, keepdims=True)
    return lax.rsqrt(squares + epsilon)


def part(which, size):
    return pl.ds(pl.multiple_of(which * size, size), size)


def pair(scale, offset, image, text, flip, image_col, text_inv, diagonal=False):
    half = text.shape[0] // 2
    raw = dot(image[:, :half], text[part(flip, half)], (1, 0)) + dot(image[:, half:], text[part(1 - flip, half)], (1, 0))
    s = raw * image_col * text_inv
    g = 1.0 / (1.0 + jnp.exp(-(scale * s + offset)))
    if diagonal:
        at = lax.broadcasted_iota(jnp.int32, g.shape, 0) == lax.broadcasted_iota(jnp.int32, g.shape, 1)
        g = g - jnp.where(at, 1.0, 0.0)
    gs = g * s
    return (
        (g * text_inv).astype(bf16),
        (g * image_col).astype(bf16),
        jnp.sum(gs, axis=1, keepdims=True),
        jnp.sum(gs, axis=0, keepdims=True),
    )


def removed(grad, hat, scale, inv, dots):
    return (grad - hat.astype(f32) * (inv * dots)) * (scale * inv)


def place():
    y = lax.axis_index("y")
    return lax.axis_index("core"), (y == 0).astype(jnp.int32), (y == lax.axis_size("y") - 1).astype(jnp.int32)


I0_INV, T0_INV, TM_INV, DOT01, C0, C1 = range(6)
IP_INV, P1_INV, P0_INV, C2, C3, C4 = range(6)


def first_kernel(log_scale, bias, t0, tm, i_own, i_far, own, i0_n, b, stats):
    half, (_, ft, _) = own.shape[0], place()
    scale, offset = jnp.exp(jnp.full((1, 1), log_scale[0], f32)), bias[0]
    i0_n[:, :half] = i_own[...].T
    i0_n[:, half:] = i_far[...].T
    i0_inv, t0_inv, tm_inv = inverse(i_own, i_far), inverse(t0), inverse(tm)
    i0_col = column(i0_inv)
    a0, b[0], r0, c0 = pair(scale, offset, i0_n, t0, 0, i0_col, t0_inv, True)
    a1, b[1], r1, c1 = pair(scale, offset, i0_n, tm, ft, i0_col, tm_inv)
    own[...] = dot(t0[:half], a0, (1, 1)) + dot(tm[part(ft, half)], a1, (1, 1))
    stats[...] = jnp.concatenate([i0_inv, t0_inv, tm_inv, row(r0 + r1), c0, c1, c0, c1], 0)


def second_kernel(
    log_scale, bias, tm, p0, p1, i_e, i_f, own, i_own, i0_n, stats,
    gi_own, gi_back, w_own, w_next, b, stats2,
    ip, ip_n,
):
    half = own.shape[0]
    core, ft, fi = place()
    scale, offset = jnp.exp(jnp.full((1, 1), log_scale[0], f32)), bias[0]
    ip[part(fi, half)] = i_e[...]
    ip[part(1 - fi, half)] = i_f[...]
    ip_n[...] = ip[...].T
    i0_inv, tm_inv, dots01 = stats[I0_INV : I0_INV + 1], stats[TM_INV : TM_INV + 1], stats[DOT01 : DOT01 + 1]
    ip_inv, p1_inv, p0_inv = inverse(ip), inverse(p1), inverse(p0)
    i0_col, ip_col = column(i0_inv), column(ip_inv)
    a2, b[0], r2, c2 = pair(scale, offset, ip_n, tm, ft, ip_col, tm_inv)
    a3, b[1], r3, c3 = pair(scale, offset, i0_n, p1, ft, i0_col, p1_inv)
    own_sum = own[...] + dot(p1[part(ft, half)], a3, (1, 1))

    def store_next(first, other, dots):
        near = removed(first(), ip[:half], scale, ip_inv, dots).astype(bf16)
        gi_back[...] = near
        w_next[...] = near

        @pl.when(fi == 1)
        def _():
            gi_back[...] = removed(other(), ip[half:], scale, ip_inv, dots).astype(bf16)

    def store_stats(c4):
        stats2[...] = jnp.concatenate([ip_inv, p1_inv, p0_inv, c2, c3, c4, c2, c3], 0)

    @pl.when(core == 0)
    def _():
        a4, b[2], r4, c4 = pair(scale, offset, ip_n, p1, ft, ip_col, p1_inv)
        whole = removed(own_sum, i_own[...], scale, i0_inv, dots01 + row(r3))
        gi_own[...] = whole
        w_own[...] = whole.astype(bf16)
        store_next(
            lambda: dot(tm[part(ft, half)], a2, (1, 1)) + dot(p1[part(ft, half)], a4, (1, 1)),
            lambda: dot(tm[part(1 - ft, half)], a2, (1, 1)) + dot(p1[part(1 - ft, half)], a4, (1, 1)),
            row(r2 + r4),
        )
        store_stats(c4)

    @pl.when(core == 1)
    def _():
        a4, b[2], r4, c4 = pair(scale, offset, i0_n, p0, 0, i0_col, p0_inv)
        whole = removed(own_sum + dot(p0[:half], a4, (1, 1)), i_own[...], scale, i0_inv, dots01 + row(r3 + r4))
        gi_own[...] = whole
        w_own[...] = whole.astype(bf16)
        store_next(
            lambda: dot(tm[part(ft, half)], a2, (1, 1)),
            lambda: dot(tm[part(1 - ft, half)], a2, (1, 1)),
            row(r2),
        )
        store_stats(c4)


def text_kernel(log_scale, t0, tm, p0, p1, i_own, i_far, i_e, i_f, b01, b234, stats, stats2, gt_own, gt_back, d_p1, d_p0):
    half = gt_own.shape[0]
    core, ft, fi = place()
    scale = jnp.exp(jnp.full((1, 1), log_scale[0], f32))
    t0_inv, tm_inv, p1_inv = stats[T0_INV : T0_INV + 1], stats[TM_INV : TM_INV + 1], stats2[P1_INV : P1_INV + 1]
    c0, c1, c2, c3, c4 = stats[C0 : C0 + 1], stats[C1 : C1 + 1], stats2[C2 : C2 + 1], stats2[C3 : C3 + 1], stats2[C4 : C4 + 1]
    gt_own[...] = removed(dot(i_own[...], b01[0], (1, 0)), t0[:half], scale, t0_inv, c0)
    own = jnp.where(ft == 1, i_far[...], i_own[...])
    next_ = jnp.where(ft == fi, i_e[...], i_f[...])
    back = dot(own, b01[1], (1, 0)) + dot(next_, b234[0], (1, 0))
    gt_back[...] = removed(back, tm[:half], scale, tm_inv, c1 + c2)
    d3 = dot(own, b234[1], (1, 0))

    @pl.when(core == 0)
    def _():
        both = d3 + dot(next_, b234[2], (1, 0))
        d_p1[...] = removed(both, p1[:half], scale, p1_inv, c3 + c4).astype(bf16)
        d_p0[...] = jnp.zeros(d_p0.shape, bf16)

    @pl.when(core == 1)
    def _():
        d_p1[...] = removed(d3, p1[:half], scale, p1_inv, c3).astype(bf16)
        d_p0[...] = removed(dot(i_own[...], b234[2], (1, 0)), p0[:half], scale, stats2[P0_INV : P0_INV + 1], c4).astype(bf16)


def local(kernel, scalars, args, outs, scratch, flops, name, limit=16):
    smem, vmem = pl.BlockSpec(memory_space=pltpu.SMEM), pl.BlockSpec(memory_space=pltpu.VMEM)
    return pl.pallas_call(
        kernel,
        out_shape=[jax.ShapeDtypeStruct(*out) for out in outs],
        in_specs=[smem] * scalars + [vmem] * (len(args) - scalars),
        out_specs=[vmem] * len(outs),
        scratch_shapes=[pltpu.VMEM(*shape) for shape in scratch],
        compiler_params=pltpu.CompilerParams(vmem_limit_bytes=limit * 2**20),
        cost_estimate=pl.CostEstimate(flops=flops, bytes_accessed=4_000_000, transcendentals=200_000),
        name=name,
    )(*args)


def weight_kernel(other, w_own, w_next, features, next_features, out):
    core, part = lax.axis_index("core"), w_own.shape[0] // 2
    at = pl.ds(pl.multiple_of((1 - core if other else core) * part, part), part)
    a, b = w_own[at], w_next[at]
    for group in range(features.shape[1] // 128):
        columns = slice(group * 128, group * 128 + 128)
        total = dot(a, features[:, columns], (1, 0)) + dot(b, next_features[:, columns], (1, 0))
        out[group * part : (group + 1) * part] = total.astype(out.dtype)
    filled = features.shape[1] // 128 * part
    out[filled:] = jnp.zeros((out.shape[0] - filled, 128), out.dtype)


def join_kernel(mine, other, out):
    core, part = lax.axis_index("core"), out.shape[0] // 2
    here = pl.ds(pl.multiple_of(core * part, part), part)
    there = pl.ds(pl.multiple_of((1 - core) * part, part), part)
    for group in range(out.shape[1] // 128):
        rows, columns = slice(group * part, (group + 1) * part), slice(group * 128, group * 128 + 128)
        out[here, columns] = mine[rows]
        out[there, columns] = other[rows]


def shards(features, img_weight, text_embed, log_scale, logit_bias):
    half, width = img_weight.shape[1], features.shape[1]
    count = features.shape[0]

    t_own = text_embed.T
    t_far = swapped(t_own, "rep")
    t_a = shifted(t_own, 2)
    i_own = lax.optimization_barrier(dot(img_weight, features, (0, 1)).astype(bf16))
    i_far = swapped(i_own, "rep")
    i_e = shifted(i_own, -2)
    t_b = swapped(lax.optimization_barrier((t_a, i_far))[0], "rep")
    next_features = shifted(lax.optimization_barrier((features, t_a))[0], -2)
    i_f = swapped(i_e, "rep")
    t0 = jnp.concatenate([t_own, t_far], 0)
    tm = jnp.concatenate([t_a, t_b], 0)
    whole, square, by_row = (half, count), (count, count), (8, count)
    own, i0_n, b01, stats = local(
        first_kernel, 2, (log_scale, logit_bias, t0, tm, i_own, i_far),
        [(whole, f32), ((count, 2 * half), bf16), ((2, *square), bf16), (by_row, f32)], [], 500_000_000, "first_pairs",
    )
    late_tm, next_features, own = lax.optimization_barrier((tm, next_features, own))
    p1 = swapped(late_tm, "core")
    p0 = lax.ppermute(t0, "core", [(0, 1)])
    gi_own, gi_back, w_own, w_next, b234, stats2 = local(
        second_kernel, 2, (log_scale, logit_bias, tm, p0, p1, i_e, i_f, own, i_own, i0_n, stats),
        [(whole, f32), (whole, bf16), (whole, bf16), (whole, bf16), ((3, *square), bf16), (by_row, f32)],
        [((2 * half, count), bf16), ((count, 2 * half), bf16)], 800_000_000, "second_pairs",
    )
    gt_own, gt_back, d_p1, d_p0 = local(
        text_kernel, 1, (log_scale, t0, tm, p0, p1, i_own, i_far, i_e, i_f, b01, b234, stats, stats2),
        [(whole, f32), (whole, f32), (whole, bf16), (whole, bf16)], [], 400_000_000, "text_gradients",
    )

    peers = lax.axis_size(PLANE)
    deep = -(-half * width // (2 * 128 * peers * 16)) * 16
    theirs, mine = (
        local(
            functools.partial(weight_kernel, other), 0, (w_own, w_next, features, next_features),
            [((peers * deep, 128), dtype)], [], 340_000_000, "weight_part", 8,
        )[0]
        for other, dtype in ((True, bf16), (False, f32))
    )
    tiles = (mine + swapped(theirs, "core").astype(f32)).astype(bf16).reshape(peers, deep, 128)
    pieces = lax.all_to_all(tiles, PLANE, 0, 0, tiled=True)
    gi_came = shifted(gi_back, 2)
    gt_sum = (gt_back + swapped(d_p1, "core").astype(f32)).astype(bf16)
    d_p0_came = lax.ppermute(d_p0, "core", [(1, 0)])
    gt_came = shifted(gt_sum, -2)
    piece = jnp.sum(pieces.astype(f32), axis=0)
    piece = (piece + swapped(piece, "xh")).astype(bf16)
    piece, gi_came, gt_came, d_p0_came = lax.optimization_barrier((piece, gi_came, gt_came, d_p0_came))
    sent = jnp.broadcast_to(piece[None], (peers, deep, 128))
    whole = lax.all_to_all(sent, PLANE, 0, 0, tiled=True).reshape(peers * deep, 128)
    image_grad = (gi_own + gi_came.astype(f32)).astype(bf16)
    text_grad = (gt_own + gt_came.astype(f32) + d_p0_came.astype(f32)).astype(bf16)
    whole, image_grad, text_grad = lax.optimization_barrier((whole, image_grad, text_grad))
    (weight_grad,) = local(join_kernel, 0, (whole, swapped(whole, "core")), [((half, width), bf16)], [], 0, "joined", 4)
    return image_grad.T, text_grad.T, weight_grad.T


def solution(mesh):
    fine = Mesh(mesh.devices.reshape(SIZES), AXES)
    in_specs = (P(DP, None), P(None, "rep"), P(DP, "rep"), P(), P())
    out_specs = (P(DP, "rep"), P(DP, "rep"), P(None, "rep"))
    return jax.shard_map(shards, mesh=fine, in_specs=in_specs, out_specs=out_specs, check_vma=False)
```
